32 devices in a mesh: leaf: 4 (over y, x), sep: 4 (over z), mode: 2 (over core).
Axes of the slice: x: 2, y: 2, z: 4, core: 2. Of those that a mesh axis runs over, the one named last changes fastest.
Arguments:
- modes: bfloat16 [128, 2048, 256], P(('leaf', 'sep'), 'mode'), may hold values from -0.125 to 0.125
- coupling: bfloat16 [128, 2048, 256], P(('leaf', 'sep'), 'mode'), may hold values from -6 to 6
- eigenvalues: float32 [128, 256], P(('leaf', 'sep'), 'mode'), may hold values from 200 to 4000
- separator_of: int32 [128, 1], P(('leaf', 'sep')), may hold values from 0 to 3; in each aligned block of 8 rows (0 to 7, 8 to 15, ...) at most 2 rows name the same one
- row_offset: int32 [128], P(('leaf', 'sep')), may hold values from 0 to 256
- stiffness: bfloat16 [4, 512, 512], P('sep', None, ('leaf', 'mode')), may hold values from -1 to 40
- start_block: bfloat16 [4, 512, 256], P('sep', ('leaf', 'mode')), may hold values from -40 to 40
- rotations: bfloat16 [4, 2, 256, 256], P('sep'), may hold values from -0.375 to 0.375
Outputs:
- subspace: bfloat16 [4, 512, 256], P('sep', ('leaf', 'mode'))
- column_norms: float32 [4, 2, 256], P('sep')
The draws below stay inside these ranges and needn't reach their ends.
Inputs may be any that keep to these rules, and one draw needn't show every extreme that they name: `separator_of`: among the 8 leaves of one device at most 2 couple to one separator, and in every draw some separator gets exactly 2 of them.
All inputs are finite; a program needn't handle non-finite values.
Results may differ from the reference program's by a relative error of at most 0.0075.
Values may be sent and summed in bfloat16 or wider, within the bound.
A program may use at most 64 MiB of HBM per device.

```python
import math
import jax
import jax.numpy as jnp
import numpy as np
from jax import lax

DOF = 2048
MODES = 256
IFACE = 256
SEP_ROWS = 512
COLS = 256
LEAF_DEV = 8
CAP = 2
ITERS = 2
NLEAF = 128
NSEP = 4


def draw_stiffness(key, part):
    split_keys = jax.random.split(key, 2)
    position = jnp.arange(SEP_ROWS, dtype=jnp.float32) / SEP_ROWS
    spread = jnp.exp(jax.random.uniform(split_keys[0], (NSEP, SEP_ROWS), jnp.float32, math.log(0.6), math.log(1.6)))
    diagonal = 2.0 * 10.0 ** position * spread
    coupled = jax.random.truncated_normal(split_keys[1], -4.0, 4.0, (NSEP, SEP_ROWS, SEP_ROWS), jnp.float32)
    coupled = coupled * (2.0 / math.sqrt(SEP_ROWS))
    identity = jnp.eye(SEP_ROWS, dtype=jnp.float32)
    return (coupled + diagonal[:, :, None] * identity[None]).astype(jnp.bfloat16)


def draw_start_block(key, part):
    split_keys = jax.random.split(key, 2)
    values = jax.random.truncated_normal(split_keys[0], -4.0, 4.0, (NSEP, SEP_ROWS, COLS), jnp.float32)
    scales = jnp.exp(jax.random.uniform(split_keys[1], (NSEP, 1, COLS), jnp.float32, 0.0, math.log(10.0)))
    return (values * scales).astype(jnp.bfloat16)


def place_ends(drawn, rng, low, top_value):
    longest = drawn.shape.index(max(drawn.shape))
    spots = []
    for shift in (0, 1):
        where = [jax.random.randint(jax.random.fold_in(rng, axis), (), 0, length) for axis, length in enumerate(drawn.shape)]
        where[longest] = (where[longest] + shift) % drawn.shape[longest]
        spots.append(tuple(where))
    return drawn.at[spots[0]].set(low).at[spots[1]].set(top_value)


def levels(rng, dims, shards, low, largest):
    def one(dim, blocks):
        steps = jax.random.uniform(jax.random.fold_in(jax.random.fold_in(rng, 6), dim), (blocks,), jnp.float32, low / len(shards), largest / len(shards))
        return jnp.repeat(jnp.exp(steps), dims[dim] // blocks).reshape((-1,) + (1,) * (len(dims) - dim - 1))

    factor_of = one(*shards[0])
    for cut in shards[1:]:
        factor_of = factor_of * one(*cut)
    return factor_of


def routed_block(own_key, own, number, rows, number_of, top, reach, skew):
    sequence = jax.random.permutation(own_key, number_of)
    heavy_load, ordinary = shares(number_of, rows * top, reach, skew, True), shares(number_of, rows * top, reach, skew, False)
    places = jnp.arange(number_of)

    def named(tallies, offset_by):
        used = int((tallies > 0).sum())
        fixed = max(1, used // 4)
        shifted = fixed + (places - fixed + offset_by * (used - fixed)) % max(1, number_of - fixed)
        return jnp.zeros((number_of,), jnp.int32).at[sequence[jnp.where(places < fixed, places, shifted)]].set(jnp.asarray(tallies, jnp.int32))

    tallies = jnp.where(number % 4 == 0, named(heavy_load, number // 4), named(ordinary, number - number // 4 - 1))
    mixed = jax.random.permutation(jax.random.fold_in(own, 3), number_of)
    giver, taker = mixed[0:number_of // 2 * 2:2], mixed[1:number_of // 2 * 2:2]
    margin = jnp.minimum(tallies[giver] - 1, reach - tallies[taker]) // 2
    margin = jnp.where((giver == sequence[0]) | (taker == sequence[0]) | (tallies[taker] == 0), 0, jnp.maximum(margin, 0))
    shifted = jax.random.randint(jax.random.fold_in(own, 4), (number_of // 2,), 0, 1 << 20) % (margin + 1)
    tallies = tallies.at[giver].add(-shifted).at[taker].add(shifted)
    items = jnp.searchsorted(jnp.cumsum(tallies), jnp.arange(rows * top), side="right").astype(jnp.int32)
    grid = items.reshape(top, rows).T
    grid = grid[jax.random.permutation(jax.random.fold_in(own, 1), rows)]
    offset_by = jax.random.randint(jax.random.fold_in(own, 2), (rows, 1), 0, top)
    return jnp.take_along_axis(grid, (jnp.arange(top)[None, :] + offset_by) % top, axis=1)


def shares(count, total, bound, lean, full):
    loads = [(1 << 20) // math.isqrt(grade ** lean) + 1 for grade in range(1, count + 1)]
    largest = bound if full else min(bound, max(-(-total // count), total * loads[0] // sum(loads)))
    least = 1 if total - largest >= count - 1 else 0
    holding, rest = [largest] + [least] * (count - 1), total - largest - least * (count - 1)
    while rest > 0:
        movable = [i for i in range(1, count) if holding[i] < largest] or [i for i in range(1, count) if holding[i] < bound]
        pool, remaining = sum([loads[i] for i in movable]), rest
        for i in movable:
            more = min(bound - holding[i], max(1, remaining * loads[i] // pool), rest)
            holding[i] = holding[i] + more
            rest = rest - more
    return np.array(holding)


def bell_draw(own_key, extent, scale, most, cuts=(), kind=jnp.bfloat16):
    level = levels(own_key, extent, cuts, -0.22, 0.18) if cuts else 1.0
    result = jax.random.normal(own_key, extent, jnp.float32) * scale * level
    return jnp.minimum(jnp.maximum(result, -most), most).astype(kind)


def setup_inputs(seed: int = 0) -> dict:
    keys = jax.random.split(jax.random.key(seed), 9)
    modes = bell_draw(keys[0], (NLEAF, DOF, MODES), DOF ** -0.5, 0.125, ((0, 16), (1, 2)))
    coupling = bell_draw(keys[1], (NLEAF, DOF, IFACE), 1.0, 6.0, ((0, 16), (1, 2)))
    eigenvalues = jnp.clip(jnp.exp(math.log(4000.0) - 2.9957323 * jax.random.uniform(keys[2], (NLEAF, MODES), jnp.float32) ** levels(keys[2], (NLEAF, MODES), ((0, 16), (1, 2)), -0.2, 0.2)), 200.0, 4000.0)
    separator_of_keys = jax.random.split(jax.random.fold_in(keys[3], 1), NLEAF // LEAF_DEV)
    separator_of_turns = jax.random.permutation(jax.random.fold_in(keys[3], 3), NLEAF // LEAF_DEV)
    separator_of = jax.vmap(lambda own, number: routed_block(jax.random.fold_in(keys[3], 2), own, number, LEAF_DEV, NSEP, 1, CAP, 2))(separator_of_keys, separator_of_turns).reshape((NLEAF, 1))
    row_offset = place_ends(jax.random.randint(keys[4], (NLEAF,), 0, SEP_ROWS - IFACE + 1), jax.random.fold_in(keys[4], 1), 0, SEP_ROWS - IFACE).astype(jnp.int32)
    stiffness = draw_stiffness(jax.random.fold_in(keys[8], 71), 0)
    start_block = draw_start_block(jax.random.fold_in(keys[8], 71), 0)
    rotations = bell_draw(keys[7], (NSEP, ITERS, COLS, COLS), COLS ** -0.5, 0.375, ((0, 4),))
    return {"modes": modes, "coupling": coupling, "eigenvalues": eigenvalues, "separator_of": separator_of, "row_offset": row_offset, "stiffness": stiffness, "start_block": start_block, "rotations": rotations}


epsilon = 1e-06

def reference(modes, coupling, eigenvalues, separator_of, row_offset, stiffness, start_block, rotations):
    highest = lax.Precision.HIGHEST

    def leaf_block(leaf_data):
        leaf_modes, leaf_coupling, leaf_eigen = leaf_data
        product = jnp.dot(leaf_coupling.T.astype(jnp.float32), leaf_modes.astype(jnp.float32), precision=highest)
        return (product / jnp.sqrt(leaf_eigen)[None, :]).astype(jnp.bfloat16)
    scaled = lax.map(leaf_block, (modes, coupling, eigenvalues))
    current = start_block
    zero_index = jnp.zeros((), jnp.int32)
    norm_list = []
    for iteration in range(ITERS):

        def add_leaf(leaf_index, accumulated):
            target = separator_of[leaf_index, 0].astype(jnp.int32)
            offset = row_offset[leaf_index].astype(jnp.int32)
            window = lax.dynamic_slice(current, (target, offset, zero_index), (1, IFACE, COLS))[0]
            weights = scaled[leaf_index].astype(jnp.float32)
            projected = jnp.dot(weights.T, window.astype(jnp.float32), precision=highest).astype(jnp.bfloat16)
            update = jnp.dot(weights, projected.astype(jnp.float32), precision=highest)
            existing = lax.dynamic_slice(accumulated, (target, offset, zero_index), (1, IFACE, COLS))
            return lax.dynamic_update_slice(accumulated, existing + update[None], (target, offset, zero_index))
        correction = lax.fori_loop(0, NLEAF, add_leaf, jnp.zeros(current.shape, jnp.float32))
        summed = jnp.einsum('srt,stc->src', stiffness.astype(jnp.float32), current.astype(jnp.float32), precision=highest) - correction
        column_scale = jnp.sqrt(lax.optimization_barrier(jnp.sum(summed * summed, 1)) / SEP_ROWS + epsilon)
        normed = (summed / column_scale[:, None, :]).astype(jnp.bfloat16)
        current = jnp.einsum('src,scd->srd', normed.astype(jnp.float32), rotations[:, iteration].astype(jnp.float32), precision=highest).astype(jnp.bfloat16)
        norm_list.append(column_scale)
    return (current, jnp.stack(norm_list, 1))
```

```python
import functools

import jax
import jax.numpy as jnp
from jax import lax
from jax.experimental import pallas as pl
from jax.experimental.pallas import tpu as pltpu
from jax.sharding import PartitionSpec as P

CAP = 2
EPSILON = 1e-06
MESH = pl.DeviceIdType.MESH
F32 = jnp.float32
BF16 = jnp.bfloat16


def remote(src, dst, send_sem, recv_sem, **device):
    return pltpu.make_async_remote_copy(
        src_ref=src,
        dst_ref=dst,
        send_sem=send_sem,
        recv_sem=recv_sem,
        device_id=device,
        device_id_type=MESH,
    )


def contract(a, b, dim_a, dim_b):
    return lax.dot_general(a, b, (((dim_a,), (dim_b,)), ((), ())), preferred_element_type=F32)


def kernel(
    nl, ns,
    separator_of, row_offset, modes_hbm, coupling_hbm, eigenvalues, stiffness, start_block, rotations,
    out, norms,
    modes, coupling, part_own, part_send, part_recv, scaled,
    slot_send, slot_recv, offset_send, offset_recv, padded,
    gram, gram_send, gram_recv, leaf_own, leaf_send, leaf_recv, operator, block, normed_rows,
    hbm_sem, part_ssem, part_rsem, block_ssem, block_rsem, slot_ssem, slot_rsem,
    offset_ssem, offset_rsem, leaf_ssem, leaf_rsem, oper_ssem, oper_rsem, core_ssem, core_rsem,
):
    leaf, sep, core = lax.axis_index("leaf"), lax.axis_index("sep"), lax.axis_index("mode")
    other = 1 - core
    leaves, _, half = scaled.shape
    iface = scaled.shape[1]
    rows = padded.shape[0]
    cols = out.shape[2]

    loads = []
    for l in range(leaves):
        pair = (
            pltpu.make_async_copy(modes_hbm.at[l], modes.at[l], hbm_sem.at[0, l]),
            pltpu.make_async_copy(coupling_hbm.at[l], coupling.at[l], hbm_sem.at[1, l]),
        )
        for copy in pair:
            copy.start()
        loads.append(pair)

    barrier = pltpu.get_barrier_semaphore()
    pl.semaphore_signal(barrier, inc=1, device_id={"mode": other}, device_id_type=MESH)
    for d in range(1, ns):
        pl.semaphore_signal(
            barrier, inc=1, device_id={"sep": lax.rem(sep + d, ns)}, device_id_type=MESH
        )
    for d in range(1, nl):
        pl.semaphore_signal(
            barrier, inc=1, device_id={"leaf": lax.rem(leaf + d, nl)}, device_id_type=MESH
        )
    pl.semaphore_wait(barrier, 1 + (ns - 1) + (nl - 1))

    block[leaf, core] = start_block[0]
    block_copies = []
    for d in range(1, nl):
        copy = remote(
            start_block.at[0], block.at[leaf, core], block_ssem.at[d], block_rsem.at[d],
            leaf=lax.rem(leaf + d, nl),
        )
        copy.start()
        block_copies.append(copy)

    part_copies = []
    for l in range(leaves):
        for copy in loads[l]:
            copy.wait()
        product = contract(coupling[l], modes[l], 0, 0)
        for k in range(2):
            piece = product[:, k * half:(k + 1) * half]
            part_own[k, l] = piece
            part_send[k, l] = piece.astype(BF16)
        copy = remote(
            part_send.at[other, l], part_recv.at[l], part_ssem.at[l], part_rsem.at[l], mode=other
        )
        copy.start()
        part_copies.append(copy)

    target = [separator_of[l, 0] for l in range(leaves)]
    position = []
    for l in range(leaves):
        count = jnp.int32(0)
        for e in range(l):
            count = count + jnp.where(target[e] == target[l], 1, 0)
        position.append(count)

    for l in range(leaves):
        part_copies[l].wait()
        summed = part_own[core, l] + part_recv[l].astype(F32)
        scaled[l] = (summed / jnp.sqrt(eigenvalues[l:l + 1, :])).astype(BF16)

    slot_copies = []
    for d in range(ns):
        owner = lax.rem(sep + d, ns)
        for p in range(CAP):
            index = jnp.int32(0)
            offset = jnp.int32(-4 * rows)
            for l in range(leaves):
                mine = (target[l] == owner) & (position[l] == p)
                index = jnp.where(mine, l, index)
                offset = jnp.where(mine, row_offset[l], offset)
            slot_send[d, p] = scaled[index]
            offset_send[d, p * 8:(p + 1) * 8, :] = jnp.full((8, iface), offset, jnp.int32)
        if d > 0:
            pair = (
                remote(offset_send.at[d], offset_recv.at[d], offset_ssem.at[d], offset_rsem.at[d], sep=owner),
                remote(slot_send.at[d], slot_recv.at[d], slot_ssem.at[d], slot_rsem.at[d], sep=owner),
            )
            for copy in pair:
                copy.start()
            slot_copies.append(pair)

    for copy in block_copies:
        copy.wait()
    block_core = remote(
        block.at[:, core], block.at[:, core], core_ssem.at[0], core_rsem.at[0], mode=other
    )
    block_core.start()

    shift = lax.broadcasted_iota(jnp.int32, (rows, iface), 0) - lax.broadcasted_iota(
        jnp.int32, (rows, iface), 1
    )
    for d in range(ns):
        if d > 0:
            for copy in slot_copies[d - 1]:
                copy.wait()
        blocks, offsets = (slot_send, offset_send) if d == 0 else (slot_recv, offset_recv)
        for p in range(CAP):
            place = jnp.where(shift == offsets[d, p * 8:p * 8 + 1, :], 1.0, 0.0).astype(BF16)
            q = d * CAP + p
            padded[:, q * half:(q + 1) * half] = jnp.dot(
                place, blocks[d, p], preferred_element_type=F32
            ).astype(BF16)
    product = contract(padded[...], padded[...], 1, 1).reshape(gram.shape)
    gram[...] = product
    gram_send[...] = product.astype(BF16)

    core_copy = remote(gram_send.at[:, other], gram_recv, core_ssem.at[1], core_rsem.at[1], mode=other)
    core_copy.start()
    core_copy.wait()
    both = gram[:, core] + gram_recv[...].astype(F32)
    leaf_own[...] = both
    leaf_send[...] = both.astype(BF16)
    leaf_copies = []
    for d in range(1, nl):
        peer = lax.rem(leaf + d, nl)
        copy = remote(leaf_send.at[peer], leaf_recv.at[d], leaf_ssem.at[d], leaf_rsem.at[d], leaf=peer)
        copy.start()
        leaf_copies.append(copy)
    total = stiffness[0].astype(F32).T - leaf_own[leaf]
    for d in range(1, nl):
        leaf_copies[d - 1].wait()
        total = total - leaf_recv[d].astype(F32)
    operator[leaf, core] = total.astype(BF16)

    oper_copies = []
    for d in range(1, nl):
        copy = remote(
            operator.at[leaf, core], operator.at[leaf, core], oper_ssem.at[d], oper_rsem.at[d],
            leaf=lax.rem(leaf + d, nl),
        )
        copy.start()
        oper_copies.append(copy)
    for copy in oper_copies:
        copy.wait()
    core_copy = remote(
        operator.at[:, core], operator.at[:, core], core_ssem.at[2], core_rsem.at[2], mode=other
    )
    core_copy.start()
    block_core.wait()
    core_copy.wait()

    turned = operator[...].reshape(rows, rows)
    current = block[...].reshape(rows, cols)
    steps = rotations.shape[1]
    for k in range(steps):
        result = contract(turned, current, 0, 0)
        column_scale = jnp.sqrt(jnp.sum(result * result, 0, keepdims=True) / rows + EPSILON)
        norms[0, k:k + 1, :] = column_scale
        normed = (result / column_scale).astype(BF16)
        if k < steps - 1:
            current = jnp.dot(normed, rotations[0, k], preferred_element_type=F32).astype(BF16)
        else:
            normed_rows[...] = normed.reshape(normed_rows.shape)
            out[0] = jnp.dot(
                normed_rows[leaf, core], rotations[0, k], preferred_element_type=F32
            ).astype(BF16)


def per_device(nl, ns, nm, modes, coupling, eigenvalues, separator_of, row_offset, stiffness, start_block, rotations):
    leaves, depth, width = modes.shape
    iface = coupling.shape[2]
    half = eigenvalues.shape[1]
    rows = stiffness.shape[1]
    own, cols = start_block.shape[1:]
    steps = rotations.shape[1]
    vmem = pl.BlockSpec(memory_space=pltpu.VMEM)
    smem = pl.BlockSpec(memory_space=pltpu.SMEM)
    hbm = pl.BlockSpec(memory_space=pl.ANY)
    dma = pltpu.SemaphoreType.DMA
    scratch = [
        pltpu.VMEM((leaves, depth, width), BF16),
        pltpu.VMEM((leaves, depth, iface), BF16),
        pltpu.VMEM((nm, leaves, iface, half), F32),
        pltpu.VMEM((nm, leaves, iface, half), BF16),
        pltpu.VMEM((leaves, iface, half), BF16),
        pltpu.VMEM((leaves, iface, half), BF16),
        pltpu.VMEM((ns, CAP, iface, half), BF16),
        pltpu.VMEM((ns, CAP, iface, half), BF16),
        pltpu.VMEM((ns, CAP * 8, iface), jnp.int32),
        pltpu.VMEM((ns, CAP * 8, iface), jnp.int32),
        pltpu.VMEM((rows, ns * CAP * half), BF16),
        pltpu.VMEM((nl, nm, own, rows), F32),
        pltpu.VMEM((nl, nm, own, rows), BF16),
        pltpu.VMEM((nl, own, rows), BF16),
        pltpu.VMEM((nl, own, rows), F32),
        pltpu.VMEM((nl, own, rows), BF16),
        pltpu.VMEM((nl, own, rows), BF16),
        pltpu.VMEM((nl, nm, own, rows), BF16),
        pltpu.VMEM((nl, nm, own, cols), BF16),
        pltpu.VMEM((nl, nm, own, cols), BF16),
        dma((2, leaves)),
        dma((leaves,)), dma((leaves,)),
        dma((nl,)), dma((nl,)),
        dma((ns,)), dma((ns,)),
        dma((ns,)), dma((ns,)),
        dma((nl,)), dma((nl,)),
        dma((nl,)), dma((nl,)),
        dma((3,)), dma((3,)),
    ]
    return pl.pallas_call(
        functools.partial(kernel, nl, ns),
        out_shape=(
            jax.ShapeDtypeStruct((1, own, cols), BF16),
            jax.ShapeDtypeStruct((1, steps, cols), F32),
        ),
        in_specs=[smem, smem, hbm, hbm, vmem, vmem, vmem, vmem],
        out_specs=(vmem, vmem),
        scratch_shapes=scratch,
        compiler_params=pltpu.CompilerParams(
            collective_id=0, has_side_effects=True, vmem_limit_bytes=48 * 1024 * 1024
        ),
    )(separator_of, row_offset, modes, coupling, eigenvalues, stiffness, start_block, rotations)


def solution(mesh):
    in_specs = (
        P(("leaf", "sep"), "mode", None),
        P(("leaf", "sep"), "mode", None),
        P(("leaf", "sep"), "mode"),
        P(("leaf", "sep"), None),
        P(("leaf", "sep")),
        P("sep", None, ("leaf", "mode")),
        P("sep", ("leaf", "mode"), None),
        P("sep", None, None, None),
    )
    out_specs = (P("sep", ("leaf", "mode"), None), P("sep", None, None))
    shape = mesh.shape
    return jax.shard_map(
        functools.partial(per_device, shape["leaf"], shape["sep"], shape["mode"]),
        mesh=mesh, in_specs=in_specs, out_specs=out_specs, check_vma=False,
    )
```

```python
import functools

import jax
import jax.numpy as jnp
from jax import lax
from jax.experimental import pallas as pl
from jax.experimental.pallas import tpu as pltpu
from jax.sharding import PartitionSpec as P

CAP = 2
EPSILON = 1e-06
MESH = pl.DeviceIdType.MESH
F32 = jnp.float32
BF16 = jnp.bfloat16


def remote(src, dst, send_sem, recv_sem, **device):
    return pltpu.make_async_remote_copy(
        src_ref=src,
        dst_ref=dst,
        send_sem=send_sem,
        recv_sem=recv_sem,
        device_id=device,
        device_id_type=MESH,
    )


def contract(a, b, dim_a, dim_b):
    return lax.dot_general(a, b, (((dim_a,), (dim_b,)), ((), ())), preferred_element_type=F32)


def partner(me, distance, count):
    if count & (count - 1):
        return lax.rem(me + distance, count)
    total = jnp.int32(0)
    bit = 1
    while bit < count:
        total = total + (me // bit + distance // bit) % 2 * bit
        bit *= 2
    return total


def kernel(
    nl, ns,
    separator_of, row_offset, modes_hbm, coupling_hbm, eigenvalues_hbm, stiffness_hbm, start_hbm, rotations_hbm,
    out, norms,
    targets, starts, eigenvalues, stiffness, start_block, rotations,
    modes, coupling, part_own, part_send, part_recv,
    slot_send, slot_recv, offset_send, offset_recv, padded,
    gram, gram_send, gram_recv, leaf_send, leaf_recv, operator, block, normed_rows,
    small_sem, hbm_sem, part_ssem, part_rsem, block_ssem, block_rsem, slot_ssem, slot_rsem,
    offset_ssem, offset_rsem, gram_ssem, gram_rsem, leaf_ssem, leaf_rsem, oper_ssem, oper_rsem,
    core_ssem, core_rsem,
):
    leaf, sep, core = lax.axis_index("leaf"), lax.axis_index("sep"), lax.axis_index("mode")
    other = 1 - core
    leaves = modes.shape[0]
    iface, half = slot_send.shape[2:]
    rows = padded.shape[0]
    own, cols = start_block.shape[1:]

    smalls = []
    for k, (src, dst) in enumerate((
        (separator_of, targets), (row_offset, starts), (start_hbm, start_block),
        (eigenvalues_hbm, eigenvalues), (stiffness_hbm, stiffness), (rotations_hbm, rotations),
    )):
        copy = pltpu.make_async_copy(src, dst, small_sem.at[k])
        copy.start()
        smalls.append(copy)
    loads = []
    for l in range(leaves):
        for k, (src, dst) in enumerate(((modes_hbm, modes), (coupling_hbm, coupling))):
            copy = pltpu.make_async_copy(src.at[l], dst.at[l], hbm_sem.at[k, l])
            copy.start()
            loads.append(copy)

    barrier = pltpu.get_barrier_semaphore()
    pl.semaphore_signal(barrier, inc=1, device_id={"mode": other}, device_id_type=MESH)
    for d in range(1, ns):
        pl.semaphore_signal(
            barrier, inc=1, device_id={"sep": partner(sep, d, ns)}, device_id_type=MESH
        )
    for d in range(1, nl):
        pl.semaphore_signal(
            barrier, inc=1, device_id={"leaf": lax.rem(leaf + d, nl)}, device_id_type=MESH
        )
    smalls[0].wait()
    smalls[1].wait()

    target = [targets[l] for l in range(leaves)]
    position = []
    for l in range(leaves):
        count = jnp.int32(0)
        for e in range(l):
            count = count + jnp.where(target[e] == target[l], 1, 0)
        position.append(count)
    order = list(range(ns // 2, ns)) + list(range(1, ns // 2)) + [0]
    slots = []
    for d in order:
        owner = partner(sep, d, ns)
        for p in range(CAP):
            index = jnp.int32(0)
            offset = jnp.int32(-4 * rows)
            for l in range(leaves):
                mine = (target[l] == owner) & (position[l] == p)
                index = jnp.where(mine, l, index)
                offset = jnp.where(mine, starts[l], offset)
            offset_send[d, p:p + 1, :] = jnp.full((1, iface), offset, jnp.int32)
            slots.append((d, p, owner, index))
    pl.semaphore_wait(barrier, 1 + (ns - 1) + (nl - 1))
    offset_copies = {}
    for d in order[:-1]:
        copy = remote(
            offset_send.at[d], offset_recv.at[d], offset_ssem.at[d], offset_rsem.at[d],
            sep=partner(sep, d, ns),
        )
        copy.start()
        offset_copies[d] = copy

    smalls[2].wait()
    block[leaf, core] = start_block[0]
    block_copies = []
    for d in range(1, nl):
        copy = remote(
            start_block.at[0], block.at[leaf, core], block_ssem.at[d], block_rsem.at[d],
            leaf=lax.rem(leaf + d, nl),
        )
        copy.start()
        block_copies.append(copy)

    smalls[3].wait()
    for copy in loads:
        copy.wait()
    part_copies = []
    slot_copies = {}

    def finish(q):
        d, p, owner, index = slots[q]
        part_copies[q].wait()
        summed = part_own[core, q] + part_recv[q].astype(F32)
        slot_send[d, p] = (summed / jnp.sqrt(eigenvalues[pl.ds(index, 1), :])).astype(BF16)
        if d > 0:
            copy = remote(
                slot_send.at[d, p], slot_recv.at[d, p], slot_ssem.at[d, p], slot_rsem.at[d, p], sep=owner
            )
            copy.start()
            slot_copies[d, p] = copy

    for q, (d, p, owner, index) in enumerate(slots):
        product = contract(coupling[index], modes[index], 0, 0)
        for k in range(2):
            piece = product[:, k * half:(k + 1) * half]
            part_own[k, q] = piece
            part_send[k, q] = piece.astype(BF16)
        copy = remote(
            part_send.at[other, q], part_recv.at[q], part_ssem.at[q], part_rsem.at[q], mode=other
        )
        copy.start()
        part_copies.append(copy)
        if q > 0:
            finish(q - 1)
    finish(len(slots) - 1)

    for copy in block_copies:
        copy.wait()
    block_core = remote(
        block.at[:, core], block.at[:, core], core_ssem.at[nl], core_rsem.at[nl], mode=other
    )
    block_core.start()

    shift = lax.broadcasted_iota(jnp.int32, (rows, iface), 0) - lax.broadcasted_iota(
        jnp.int32, (rows, iface), 1
    )
    for d in [0] + order[:-1]:
        blocks, offsets = (slot_send, offset_send) if d == 0 else (slot_recv, offset_recv)
        if d > 0:
            offset_copies[d].wait()
        for p in range(CAP):
            if d > 0:
                slot_copies[d, p].wait()
            place = jnp.where(shift == offsets[d, p:p + 1, :], 1.0, 0.0).astype(BF16)
            q = d * CAP + p
            padded[:, q * half:(q + 1) * half] = jnp.dot(
                place, blocks[d, p], preferred_element_type=F32
            ).astype(BF16)

    gram_copies = []
    peers = [lax.rem(leaf + d, nl) for d in list(range(1, nl)) + [0]]
    pair_rows = 2 * own
    for d, peer in enumerate(peers):
        chunk = padded[pl.ds(pl.multiple_of(peer * pair_rows, pair_rows), pair_rows), :]
        product = contract(chunk, padded[...], 1, 1).reshape(2, own, rows)
        gram[d] = product
        gram_send[d] = product.astype(BF16)
        copy = remote(
            gram_send.at[d, other], gram_recv.at[d], gram_ssem.at[d], gram_rsem.at[d], mode=other
        )
        copy.start()
        gram_copies.append(copy)
    leaf_copies = []
    for d, peer in enumerate(peers[:-1]):
        gram_copies[d].wait()
        leaf_send[d] = (gram[d, core] + gram_recv[d].astype(F32)).astype(BF16)
        copy = remote(leaf_send.at[d], leaf_recv.at[d], leaf_ssem.at[d], leaf_rsem.at[d], leaf=peer)
        copy.start()
        leaf_copies.append(copy)
    smalls[4].wait()
    gram_copies[nl - 1].wait()
    total = stiffness[0].astype(F32) - (gram[nl - 1, core] + gram_recv[nl - 1].astype(F32))
    for d in range(nl - 1):
        leaf_copies[d].wait()
        total = total - leaf_recv[d].astype(F32)
    operator[leaf, core] = total.astype(BF16)

    oper_copies = []
    for d in range(1, nl):
        copy = remote(
            operator.at[leaf, core], operator.at[leaf, core], oper_ssem.at[d], oper_rsem.at[d],
            leaf=lax.rem(leaf + d, nl),
        )
        copy.start()
        oper_copies.append(copy)
    core_copies = []
    for d in range(nl):
        if d > 0:
            oper_copies[d - 1].wait()
        source = lax.rem(leaf - d + nl, nl)
        copy = remote(
            operator.at[source, core], operator.at[source, core], core_ssem.at[d], core_rsem.at[d], mode=other
        )
        copy.start()
        core_copies.append(copy)
    block_core.wait()
    smalls[5].wait()
    for copy in core_copies:
        copy.wait()

    turned = operator[...].reshape(rows, rows).T
    current = block[...].reshape(rows, cols)
    steps = rotations.shape[1]
    for k in range(steps):
        result = jnp.dot(turned, current, preferred_element_type=F32)
        column_scale = jnp.sqrt(jnp.sum(result * result, 0, keepdims=True) / rows + EPSILON)
        norms[0, k:k + 1, :] = column_scale
        normed = (result / column_scale).astype(BF16)
        if k < steps - 1:
            current = jnp.dot(normed, rotations[0, k], preferred_element_type=F32).astype(BF16)
        else:
            normed_rows[...] = normed.reshape(normed_rows.shape)
            out[0] = jnp.dot(
                normed_rows[leaf, core], rotations[0, k], preferred_element_type=F32
            ).astype(BF16)


def per_device(nl, ns, nm, modes, coupling, eigenvalues, separator_of, row_offset, stiffness, start_block, rotations):
    leaves, depth, width = modes.shape
    iface = coupling.shape[2]
    half = eigenvalues.shape[1]
    rows = stiffness.shape[1]
    own, cols = start_block.shape[1:]
    steps = rotations.shape[1]
    vmem = pl.BlockSpec(memory_space=pltpu.VMEM)
    hbm = pl.BlockSpec(memory_space=pl.ANY)
    dma = pltpu.SemaphoreType.DMA
    slots = ns * CAP
    scratch = [
        pltpu.SMEM((leaves,), jnp.int32),
        pltpu.SMEM((leaves,), jnp.int32),
        pltpu.VMEM((leaves, half), F32),
        pltpu.VMEM((1, own, rows), BF16),
        pltpu.VMEM((1, own, cols), BF16),
        pltpu.VMEM((1, steps, cols, cols), BF16),
        pltpu.VMEM((leaves, depth, width), BF16),
        pltpu.VMEM((leaves, depth, iface), BF16),
        pltpu.VMEM((nm, slots, iface, half), F32),
        pltpu.VMEM((nm, slots, iface, half), BF16),
        pltpu.VMEM((slots, iface, half), BF16),
        pltpu.VMEM((ns, CAP, iface, half), BF16),
        pltpu.VMEM((ns, CAP, iface, half), BF16),
        pltpu.VMEM((ns, 8, iface), jnp.int32),
        pltpu.VMEM((ns, 8, iface), jnp.int32),
        pltpu.VMEM((rows, slots * half), BF16),
        pltpu.VMEM((nl, nm, own, rows), F32),
        pltpu.VMEM((nl, nm, own, rows), BF16),
        pltpu.VMEM((nl, own, rows), BF16),
        pltpu.VMEM((nl, own, rows), BF16),
        pltpu.VMEM((nl, own, rows), BF16),
        pltpu.VMEM((nl, nm, own, rows), BF16),
        pltpu.VMEM((nl, nm, own, cols), BF16),
        pltpu.VMEM((nl, nm, own, cols), BF16),
        dma((6,)),
        dma((2, leaves)),
        dma((slots,)), dma((slots,)),
        dma((nl,)), dma((nl,)),
        dma((ns, CAP)), dma((ns, CAP)),
        dma((ns,)), dma((ns,)),
        dma((nl,)), dma((nl,)),
        dma((nl,)), dma((nl,)),
        dma((nl,)), dma((nl,)),
        dma((nl + 1,)), dma((nl + 1,)),
    ]
    return pl.pallas_call(
        functools.partial(kernel, nl, ns),
        out_shape=(
            jax.ShapeDtypeStruct((1, own, cols), BF16),
            jax.ShapeDtypeStruct((1, steps, cols), F32),
        ),
        in_specs=[hbm] * 8,
        out_specs=(vmem, vmem),
        scratch_shapes=scratch,
        compiler_params=pltpu.CompilerParams(
            collective_id=0, has_side_effects=True, vmem_limit_bytes=60 * 1024 * 1024
        ),
    )(
        separator_of.reshape(leaves), row_offset, modes, coupling, eigenvalues,
        jnp.swapaxes(stiffness, 1, 2), start_block, rotations,
    )


def solution(mesh):
    in_specs = (
        P(("leaf", "sep"), "mode", None),
        P(("leaf", "sep"), "mode", None),
        P(("leaf", "sep"), "mode"),
        P(("leaf", "sep"), None),
        P(("leaf", "sep")),
        P("sep", None, ("leaf", "mode")),
        P("sep", ("leaf", "mode"), None),
        P("sep", None, None, None),
    )
    out_specs = (P("sep", ("leaf", "mode"), None), P("sep", None, None))
    shape = mesh.shape
    return jax.shard_map(
        functools.partial(per_device, shape["leaf"], shape["sep"], shape["mode"]),
        mesh=mesh, in_specs=in_specs, out_specs=out_specs, check_vma=False,
    )
```

```python
import functools

import jax
import jax.numpy as jnp
from jax import lax
from jax.experimental import pallas as pl
from jax.experimental.pallas import tpu as pltpu
from jax.sharding import PartitionSpec as P

CAP = 2
EPSILON = 1e-06
MESH = pl.DeviceIdType.MESH
F32 = jnp.float32
BF16 = jnp.bfloat16


def remote(src, dst, send_sem, recv_sem, **device):
    return pltpu.make_async_remote_copy(
        src_ref=src,
        dst_ref=dst,
        send_sem=send_sem,
        recv_sem=recv_sem,
        device_id=device,
        device_id_type=MESH,
    )


def contract(a, b, dim_a, dim_b):
    return lax.dot_general(a, b, (((dim_a,), (dim_b,)), ((), ())), preferred_element_type=F32)


def partner(me, distance, count):
    if count & (count - 1):
        return lax.rem(me + distance, count)
    total = jnp.int32(0)
    bit = 1
    while bit < count:
        total = total + (me // bit + distance // bit) % 2 * bit
        bit *= 2
    return total


def kernel(
    nl, ns,
    separator_of, row_offset, modes_hbm, coupling_hbm, eigenvalues_hbm, stiffness_hbm, start_hbm, rotations_hbm,
    out, norms,
    targets, starts, eigenvalues, stiffness, start_block, rotations,
    modes, coupling, eigen_both, part_send, part_recv, scales,
    slot_send, slot_recv, offset_send, offset_recv, placed, places,
    gram, gram_send, gram_recv, leaf_send, leaf_recv, operator, block, normed_rows,
    small_sem, hbm_sem, part_ssem, part_rsem, block_ssem, block_rsem, slot_ssem, slot_rsem,
    offset_ssem, offset_rsem, gram_ssem, gram_rsem, leaf_ssem, leaf_rsem, oper_ssem, oper_rsem,
    core_ssem, core_rsem, eigen_ssem, eigen_rsem,
):
    leaf, sep, core = lax.axis_index("leaf"), lax.axis_index("sep"), lax.axis_index("mode")
    other = 1 - core
    leaves = modes.shape[0]
    iface = coupling.shape[2]
    tile = iface // 2
    half = eigenvalues.shape[1]
    rows = placed.shape[0]
    own, cols = start_block.shape[1:]

    smalls = []
    for k, (src, dst) in enumerate((
        (separator_of, targets), (row_offset, starts), (start_hbm, start_block),
        (eigenvalues_hbm, eigenvalues), (stiffness_hbm, stiffness), (rotations_hbm, rotations),
    )):
        copy = pltpu.make_async_copy(src, dst, small_sem.at[k])
        copy.start()
        smalls.append(copy)
    loads = []
    for l in range(leaves):
        for k, (src, dst) in enumerate(((modes_hbm, modes), (coupling_hbm, coupling))):
            copy = pltpu.make_async_copy(src.at[l], dst.at[l], hbm_sem.at[k, l])
            copy.start()
            loads.append(copy)

    barrier = pltpu.get_barrier_semaphore()
    pl.semaphore_signal(barrier, inc=1, device_id={"mode": other}, device_id_type=MESH)
    for d in range(1, ns):
        pl.semaphore_signal(
            barrier, inc=1, device_id={"sep": partner(sep, d, ns)}, device_id_type=MESH
        )
    for d in range(1, nl):
        pl.semaphore_signal(
            barrier, inc=1, device_id={"leaf": lax.rem(leaf + d, nl)}, device_id_type=MESH
        )
    smalls[0].wait()
    smalls[1].wait()

    target = [targets[l] for l in range(leaves)]
    position = []
    for l in range(leaves):
        count = jnp.int32(0)
        for e in range(l):
            count = count + jnp.where(target[e] == target[l], 1, 0)
        position.append(count)
    order = list(range(ns // 2, ns)) + list(range(1, ns // 2)) + [0]
    slots = []
    for d in order:
        owner = partner(sep, d, ns)
        found = []
        for p in (other, core):
            index = jnp.int32(0)
            offset = jnp.int32(-4 * rows)
            for l in range(leaves):
                mine = (target[l] == owner) & (position[l] == p)
                index = jnp.where(mine, l, index)
                offset = jnp.where(mine, starts[l], offset)
            found.append(index)
        offset_send[d] = jnp.full(offset_send.shape[1:], offset, jnp.int32)
        slots.append((d, owner, found[0], found[1]))
    pl.semaphore_wait(barrier, 1 + (ns - 1) + (nl - 1))
    offset_copies = {}
    for d in order[:-1]:
        copy = remote(
            offset_send.at[d], offset_recv.at[d], offset_ssem.at[d], offset_rsem.at[d],
            sep=partner(sep, d, ns),
        )
        copy.start()
        offset_copies[d] = copy

    smalls[2].wait()
    block[leaf, core] = start_block[0]
    block_copies = []
    for d in range(1, nl):
        copy = remote(
            start_block.at[0], block.at[leaf, core], block_ssem.at[d], block_rsem.at[d],
            leaf=lax.rem(leaf + d, nl),
        )
        copy.start()
        block_copies.append(copy)

    smalls[3].wait()
    eigen_both[core] = eigenvalues[...]
    eigen_copy = remote(eigenvalues, eigen_both.at[core], eigen_ssem, eigen_rsem, mode=other)
    eigen_copy.start()

    for copy in loads:
        copy.wait()
    eigen_copy.wait()
    for k in range(2):
        scales[:, k * half:(k + 1) * half] = 1.0 / jnp.sqrt(eigen_both[k])
    slot_copies = {}
    for d, owner, given, kept in slots:
        part_send[d] = contract(coupling[given], modes[given], 0, 0).astype(BF16)
        part_copy = remote(part_send.at[d], part_recv.at[d], part_ssem.at[d], part_rsem.at[d], mode=other)
        part_copy.start()
        product = contract(coupling[kept], modes[kept], 0, 0)
        part_copy.wait()
        scaled = ((product + part_recv[d].astype(F32)) * scales[pl.ds(kept, 1), :]).astype(BF16)
        square = contract(scaled, scaled, 1, 1).astype(BF16)
        slot_send[d, 0] = square[:tile, :tile]
        slot_send[d, 1] = square[tile:, :tile]
        slot_send[d, 2] = square[tile:, tile:]
        if d > 0:
            copy = remote(slot_send.at[d], slot_recv.at[d], slot_ssem.at[d], slot_rsem.at[d], sep=owner)
            copy.start()
            slot_copies[d] = copy

    for copy in block_copies:
        copy.wait()
    block_core = remote(
        block.at[:, core], block.at[:, core], core_ssem.at[nl], core_rsem.at[nl], mode=other
    )
    block_core.start()

    shift = lax.broadcasted_iota(jnp.int32, (rows, iface), 0) - lax.broadcasted_iota(
        jnp.int32, (rows, iface), 1
    )
    for d in [0] + order[:-1]:
        blocks, offsets = (slot_send, offset_send) if d == 0 else (slot_recv, offset_recv)
        if d > 0:
            offset_copies[d].wait()
        place = jnp.where(shift == offsets[d, 0:1, :], 1.0, 0.0).astype(BF16)
        places[:, d * iface:(d + 1) * iface] = place
        if d > 0:
            slot_copies[d].wait()
        corner = blocks[d, 1]
        top = jnp.concatenate([blocks[d, 0], corner.T], axis=1)
        low = jnp.concatenate([corner, blocks[d, 2]], axis=1)
        placed[:, d * iface:(d + 1) * iface] = (
            jnp.dot(place[:, :tile], top, preferred_element_type=F32)
            + jnp.dot(place[:, tile:], low, preferred_element_type=F32)
        ).astype(BF16)

    gram_copies = []
    peers = [lax.rem(leaf + d, nl) for d in list(range(1, nl)) + [0]]
    pair_rows = 2 * own
    for d, peer in enumerate(peers):
        chunk = placed[pl.ds(pl.multiple_of(peer * pair_rows, pair_rows), pair_rows), :]
        product = contract(chunk, places[...], 1, 1).reshape(2, own, rows)
        gram[d] = product
        gram_send[d] = product.astype(BF16)
        copy = remote(
            gram_send.at[d, other], gram_recv.at[d], gram_ssem.at[d], gram_rsem.at[d], mode=other
        )
        copy.start()
        gram_copies.append(copy)
    leaf_copies = []
    for d, peer in enumerate(peers[:-1]):
        gram_copies[d].wait()
        leaf_send[d] = (gram[d, core] + gram_recv[d].astype(F32)).astype(BF16)
        copy = remote(leaf_send.at[d], leaf_recv.at[d], leaf_ssem.at[d], leaf_rsem.at[d], leaf=peer)
        copy.start()
        leaf_copies.append(copy)
    smalls[4].wait()
    gram_copies[nl - 1].wait()
    total = stiffness[0].astype(F32) - (gram[nl - 1, core] + gram_recv[nl - 1].astype(F32))
    for d in range(nl - 1):
        leaf_copies[d].wait()
        total = total - leaf_recv[d].astype(F32)
    operator[leaf, core] = total.astype(BF16)

    oper_copies = []
    for d in range(1, nl):
        copy = remote(
            operator.at[leaf, core], operator.at[leaf, core], oper_ssem.at[d], oper_rsem.at[d],
            leaf=lax.rem(leaf + d, nl),
        )
        copy.start()
        oper_copies.append(copy)
    core_copies = []
    for d in range(nl):
        if d > 0:
            oper_copies[d - 1].wait()
        source = lax.rem(leaf - d + nl, nl)
        copy = remote(
            operator.at[source, core], operator.at[source, core], core_ssem.at[d], core_rsem.at[d], mode=other
        )
        copy.start()
        core_copies.append(copy)
    block_core.wait()
    smalls[5].wait()
    for copy in core_copies:
        copy.wait()

    turned = operator[...].reshape(rows, rows).T
    current = block[...].reshape(rows, cols)
    steps = rotations.shape[1]
    for k in range(steps):
        result = jnp.dot(turned, current, preferred_element_type=F32)
        column_scale = jnp.sqrt(jnp.sum(result * result, 0, keepdims=True) / rows + EPSILON)
        norms[0, k:k + 1, :] = column_scale
        normed = (result * (1.0 / column_scale)).astype(BF16)
        if k < steps - 1:
            current = jnp.dot(normed, rotations[0, k], preferred_element_type=F32).astype(BF16)
        else:
            normed_rows[...] = normed.reshape(normed_rows.shape)
            out[0] = jnp.dot(
                normed_rows[leaf, core], rotations[0, k], preferred_element_type=F32
            ).astype(BF16)


def per_device(nl, ns, nm, modes, coupling, eigenvalues, separator_of, row_offset, stiffness, start_block, rotations):
    leaves, depth, width = modes.shape
    iface = coupling.shape[2]
    half = eigenvalues.shape[1]
    rows = stiffness.shape[1]
    own, cols = start_block.shape[1:]
    steps = rotations.shape[1]
    vmem = pl.BlockSpec(memory_space=pltpu.VMEM)
    hbm = pl.BlockSpec(memory_space=pl.ANY)
    dma = pltpu.SemaphoreType.DMA
    assert nm == CAP
    scratch = [
        pltpu.SMEM((leaves,), jnp.int32),
        pltpu.SMEM((leaves,), jnp.int32),
        pltpu.VMEM((leaves, half), F32),
        pltpu.VMEM((1, own, rows), BF16),
        pltpu.VMEM((1, own, cols), BF16),
        pltpu.VMEM((1, steps, cols, cols), BF16),
        pltpu.VMEM((leaves, depth, width), BF16),
        pltpu.VMEM((leaves, depth, iface), BF16),
        pltpu.VMEM((nm, leaves, half), F32),
        pltpu.VMEM((ns, iface, width), BF16),
        pltpu.VMEM((ns, iface, width), BF16),
        pltpu.VMEM((leaves, width), F32),
        pltpu.VMEM((ns, 3, iface // 2, iface // 2), BF16),
        pltpu.VMEM((ns, 3, iface // 2, iface // 2), BF16),
        pltpu.VMEM((ns, 8, iface), jnp.int32),
        pltpu.VMEM((ns, 8, iface), jnp.int32),
        pltpu.VMEM((rows, ns * iface), BF16),
        pltpu.VMEM((rows, ns * iface), BF16),
        pltpu.VMEM((nl, nm, own, rows), F32),
        pltpu.VMEM((nl, nm, own, rows), BF16),
        pltpu.VMEM((nl, own, rows), BF16),
        pltpu.VMEM((nl, own, rows), BF16),
        pltpu.VMEM((nl, own, rows), BF16),
        pltpu.VMEM((nl, nm, own, rows), BF16),
        pltpu.VMEM((nl, nm, own, cols), BF16),
        pltpu.VMEM((nl, nm, own, cols), BF16),
        dma((6,)),
        dma((2, leaves)),
        dma((ns,)), dma((ns,)),
        dma((nl,)), dma((nl,)),
        dma((ns,)), dma((ns,)),
        dma((ns,)), dma((ns,)),
        dma((nl,)), dma((nl,)),
        dma((nl,)), dma((nl,)),
        dma((nl,)), dma((nl,)),
        dma((nl + 1,)), dma((nl + 1,)),
        dma, dma,
    ]
    return pl.pallas_call(
        functools.partial(kernel, nl, ns),
        out_shape=(
            jax.ShapeDtypeStruct((1, own, cols), BF16),
            jax.ShapeDtypeStruct((1, steps, cols), F32),
        ),
        in_specs=[hbm] * 8,
        out_specs=(vmem, vmem),
        scratch_shapes=scratch,
        compiler_params=pltpu.CompilerParams(
            collective_id=0, has_side_effects=True, vmem_limit_bytes=60 * 1024 * 1024
        ),
    )(
        separator_of.reshape(leaves), row_offset, modes, coupling, eigenvalues,
        jnp.swapaxes(stiffness, 1, 2), start_block, rotations,
    )


def solution(mesh):
    in_specs = (
        P(("leaf", "sep"), "mode", None),
        P(("leaf", "sep"), "mode", None),
        P(("leaf", "sep"), "mode"),
        P(("leaf", "sep"), None),
        P(("leaf", "sep")),
        P("sep", None, ("leaf", "mode")),
        P("sep", ("leaf", "mode"), None),
        P("sep", None, None, None),
    )
    out_specs = (P("sep", ("leaf", "mode"), None), P("sep", None, None))
    shape = mesh.shape
    return jax.shard_map(
        functools.partial(per_device, shape["leaf"], shape["sep"], shape["mode"]),
        mesh=mesh, in_specs=in_specs, out_specs=out_specs, check_vma=False,
    )
```

```python
import functools

import jax
import jax.numpy as jnp
from jax import lax
from jax.experimental import pallas as pl
from jax.experimental.pallas import tpu as pltpu
from jax.sharding import PartitionSpec as P

CAP = 2
EPSILON = 1e-06
MESH = pl.DeviceIdType.MESH
F32 = jnp.float32
BF16 = jnp.bfloat16


def remote(src, dst, send_sem, recv_sem, **device):
    return pltpu.make_async_remote_copy(
        src_ref=src,
        dst_ref=dst,
        send_sem=send_sem,
        recv_sem=recv_sem,
        device_id=device,
        device_id_type=MESH,
    )


def contract(a, b, dim_a, dim_b):
    return lax.dot_general(a, b, (((dim_a,), (dim_b,)), ((), ())), preferred_element_type=F32)


def partner(me, distance, count):
    if count & (count - 1):
        return lax.rem(me + distance, count)
    total = jnp.int32(0)
    bit = 1
    while bit < count:
        total = total + (me // bit + distance // bit) % 2 * bit
        bit *= 2
    return total


def kernel(
    nl, ns,
    separator_of, row_offset, modes_hbm, coupling_hbm, eigenvalues_hbm, stiffness_hbm, start_hbm, rotations_hbm,
    out, norms,
    targets, starts, eigenvalues, stiffness, start_block, rotations,
    modes, coupling, eigen_both, part_send, part_recv, scales,
    slot_send, slot_recv, offset_send, offset_recv, placed, places,
    gram, gram_send, gram_recv, leaf_send, leaf_recv, operator, block, normed_rows,
    small_sem, hbm_sem, part_ssem, part_rsem, block_ssem, block_rsem, slot_ssem, slot_rsem,
    offset_ssem, offset_rsem, gram_ssem, gram_rsem, leaf_ssem, leaf_rsem, oper_ssem, oper_rsem,
    core_ssem, core_rsem, eigen_ssem, eigen_rsem,
):
    leaf, sep, core = lax.axis_index("leaf"), lax.axis_index("sep"), lax.axis_index("mode")
    other = 1 - core
    leaves = modes.shape[0]
    iface = coupling.shape[2]
    tile = iface // 2
    half = eigenvalues.shape[1]
    rows = placed.shape[0]
    own, cols = start_block.shape[1:]

    smalls = []
    for k, (src, dst) in enumerate((
        (separator_of, targets), (row_offset, starts), (start_hbm, start_block),
        (eigenvalues_hbm, eigenvalues), (stiffness_hbm, stiffness), (rotations_hbm, rotations),
    )):
        copy = pltpu.make_async_copy(src, dst, small_sem.at[k])
        copy.start()
        smalls.append(copy)
    loads = []
    for l in range(leaves):
        for k, (src, dst) in enumerate(((modes_hbm, modes), (coupling_hbm, coupling))):
            copy = pltpu.make_async_copy(src.at[l], dst.at[l], hbm_sem.at[k, l])
            copy.start()
            loads.append(copy)

    barrier = pltpu.get_barrier_semaphore()
    pl.semaphore_signal(barrier, inc=1, device_id={"mode": other}, device_id_type=MESH)
    for d in range(1, ns):
        pl.semaphore_signal(
            barrier, inc=1, device_id={"sep": partner(sep, d, ns)}, device_id_type=MESH
        )
    for d in range(1, nl):
        pl.semaphore_signal(
            barrier, inc=1, device_id={"leaf": lax.rem(leaf + d, nl)}, device_id_type=MESH
        )
    smalls[0].wait()
    smalls[1].wait()

    target = [targets[l] for l in range(leaves)]
    position = []
    for l in range(leaves):
        count = jnp.int32(0)
        for e in range(l):
            count = count + jnp.where(target[e] == target[l], 1, 0)
        position.append(count)
    order = list(range(ns // 2, ns)) + list(range(1, ns // 2)) + [0]
    slots = []
    for d in order:
        owner = partner(sep, d, ns)
        found = []
        for p in (other, core):
            index = jnp.int32(0)
            offset = jnp.int32(-4 * rows)
            for l in range(leaves):
                mine = (target[l] == owner) & (position[l] == p)
                index = jnp.where(mine, l, index)
                offset = jnp.where(mine, starts[l], offset)
            found.append(index)
        offset_send[d] = jnp.full(offset_send.shape[1:], offset, jnp.int32)
        slots.append((d, owner, found[0], found[1]))
    pl.semaphore_wait(barrier, 1 + (ns - 1) + (nl - 1))
    offset_copies = {}
    for d in order[:-1]:
        copy = remote(
            offset_send.at[d], offset_recv.at[d], offset_ssem.at[d], offset_rsem.at[d],
            sep=partner(sep, d, ns),
        )
        copy.start()
        offset_copies[d] = copy

    smalls[2].wait()
    block[leaf, core] = start_block[0]
    block_copies = []
    for d in range(1, nl):
        copy = remote(
            start_block.at[0], block.at[leaf, core], block_ssem.at[d], block_rsem.at[d],
            leaf=lax.rem(leaf + d, nl),
        )
        copy.start()
        block_copies.append(copy)

    smalls[3].wait()
    eigen_both[core] = eigenvalues[...]
    eigen_copy = remote(eigenvalues, eigen_both.at[core], eigen_ssem, eigen_rsem, mode=other)
    eigen_copy.start()

    for copy in loads:
        copy.wait()
    eigen_copy.wait()
    for k in range(2):
        scales[:, k * half:(k + 1) * half] = 1.0 / jnp.sqrt(eigen_both[k])
    slot_copies = {}
    part_copies = {}

    def give(d, owner, given, kept):
        part_send[d] = contract(coupling[given], modes[given], 0, 0).astype(BF16)
        copy = remote(part_send.at[d], part_recv.at[d], part_ssem.at[d], part_rsem.at[d], mode=other)
        copy.start()
        part_copies[d] = copy

    give(*slots[0])
    for step, (d, owner, given, kept) in enumerate(slots):
        product = contract(coupling[kept], modes[kept], 0, 0)
        if step + 1 < len(slots):
            give(*slots[step + 1])
        part_copies[d].wait()
        scaled = ((product + part_recv[d].astype(F32)) * scales[pl.ds(kept, 1), :]).astype(BF16)
        square = contract(scaled, scaled, 1, 1).astype(BF16)
        slot_send[d, 0] = square[:tile, :tile]
        slot_send[d, 1] = square[tile:, :tile]
        slot_send[d, 2] = square[tile:, tile:]
        if d > 0:
            copy = remote(slot_send.at[d], slot_recv.at[d], slot_ssem.at[d], slot_rsem.at[d], sep=owner)
            copy.start()
            slot_copies[d] = copy

    for copy in block_copies:
        copy.wait()
    block_core = remote(
        block.at[:, core], block.at[:, core], core_ssem.at[nl], core_rsem.at[nl], mode=other
    )
    block_core.start()

    shift = lax.broadcasted_iota(jnp.int32, (rows, iface), 0) - lax.broadcasted_iota(
        jnp.int32, (rows, iface), 1
    )
    turned_shift = lax.broadcasted_iota(jnp.int32, (iface, rows), 1) - lax.broadcasted_iota(
        jnp.int32, (iface, rows), 0
    )
    for d in [0] + order[:-1]:
        blocks, offsets = (slot_send, offset_send) if d == 0 else (slot_recv, offset_recv)
        if d > 0:
            offset_copies[d].wait()
        place = jnp.where(shift == offsets[d, 0:1, :iface], 1.0, 0.0).astype(BF16)
        places[d * iface:(d + 1) * iface, :] = jnp.where(
            turned_shift == offsets[d, 0:1, :], 1.0, 0.0
        ).astype(BF16)
        if d > 0:
            slot_copies[d].wait()
        corner = blocks[d, 1]
        top = jnp.concatenate([blocks[d, 0], corner.T], axis=1)
        low = jnp.concatenate([corner, blocks[d, 2]], axis=1)
        placed[:, d * iface:(d + 1) * iface] = (
            jnp.dot(place[:, :tile], top, preferred_element_type=F32)
            + jnp.dot(place[:, tile:], low, preferred_element_type=F32)
        ).astype(BF16)

    gram_copies = []
    peers = [lax.rem(leaf + d, nl) for d in list(range(1, nl)) + [0]]
    pair_rows = 2 * own
    for d, peer in enumerate(peers):
        chunk = placed[pl.ds(pl.multiple_of(peer * pair_rows, pair_rows), pair_rows), :]
        product = jnp.dot(chunk, places[...], preferred_element_type=F32).reshape(2, own, rows)
        gram[d] = product
        gram_send[d] = product.astype(BF16)
        copy = remote(
            gram_send.at[d, other], gram_recv.at[d], gram_ssem.at[d], gram_rsem.at[d], mode=other
        )
        copy.start()
        gram_copies.append(copy)
    leaf_copies = []
    for d, peer in enumerate(peers[:-1]):
        gram_copies[d].wait()
        leaf_send[d] = (gram[d, core] + gram_recv[d].astype(F32)).astype(BF16)
        copy = remote(leaf_send.at[d], leaf_recv.at[d], leaf_ssem.at[d], leaf_rsem.at[d], leaf=peer)
        copy.start()
        leaf_copies.append(copy)
    smalls[4].wait()
    gram_copies[nl - 1].wait()
    total = stiffness[0].astype(F32) - (gram[nl - 1, core] + gram_recv[nl - 1].astype(F32))
    for d in range(nl - 1):
        leaf_copies[d].wait()
        total = total - leaf_recv[d].astype(F32)
    operator[leaf, core] = total.astype(BF16)

    oper_copies = []
    for d in range(1, nl):
        copy = remote(
            operator.at[leaf, core], operator.at[leaf, core], oper_ssem.at[d], oper_rsem.at[d],
            leaf=lax.rem(leaf + d, nl),
        )
        copy.start()
        oper_copies.append(copy)
    core_copies = []
    for d in range(nl):
        if d > 0:
            oper_copies[d - 1].wait()
        source = lax.rem(leaf - d + nl, nl)
        copy = remote(
            operator.at[source, core], operator.at[source, core], core_ssem.at[d], core_rsem.at[d], mode=other
        )
        copy.start()
        core_copies.append(copy)
    block_core.wait()
    smalls[5].wait()
    for copy in core_copies:
        copy.wait()

    turned = operator[...].reshape(rows, rows).T
    current = block[...].reshape(rows, cols)
    steps = rotations.shape[1]
    for k in range(steps):
        result = jnp.dot(turned, current, preferred_element_type=F32)
        column_scale = jnp.sqrt(jnp.sum(result * result, 0, keepdims=True) / rows + EPSILON)
        norms[0, k:k + 1, :] = column_scale
        normed = (result * (1.0 / column_scale)).astype(BF16)
        if k < steps - 1:
            current = jnp.dot(normed, rotations[0, k], preferred_element_type=F32).astype(BF16)
        else:
            normed_rows[...] = normed.reshape(normed_rows.shape)
            out[0] = jnp.dot(
                normed_rows[leaf, core], rotations[0, k], preferred_element_type=F32
            ).astype(BF16)


def per_device(nl, ns, nm, modes, coupling, eigenvalues, separator_of, row_offset, stiffness, start_block, rotations):
    leaves, depth, width = modes.shape
    iface = coupling.shape[2]
    half = eigenvalues.shape[1]
    rows = stiffness.shape[1]
    own, cols = start_block.shape[1:]
    steps = rotations.shape[1]
    vmem = pl.BlockSpec(memory_space=pltpu.VMEM)
    hbm = pl.BlockSpec(memory_space=pl.ANY)
    dma = pltpu.SemaphoreType.DMA
    assert nm == CAP
    scratch = [
        pltpu.SMEM((leaves,), jnp.int32),
        pltpu.SMEM((leaves,), jnp.int32),
        pltpu.VMEM((leaves, half), F32),
        pltpu.VMEM((1, own, rows), BF16),
        pltpu.VMEM((1, own, cols), BF16),
        pltpu.VMEM((1, steps, cols, cols), BF16),
        pltpu.VMEM((leaves, depth, width), BF16),
        pltpu.VMEM((leaves, depth, iface), BF16),
        pltpu.VMEM((nm, leaves, half), F32),
        pltpu.VMEM((ns, iface, width), BF16),
        pltpu.VMEM((ns, iface, width), BF16),
        pltpu.VMEM((leaves, width), F32),
        pltpu.VMEM((ns, 3, iface // 2, iface // 2), BF16),
        pltpu.VMEM((ns, 3, iface // 2, iface // 2), BF16),
        pltpu.VMEM((ns, 8, rows), jnp.int32),
        pltpu.VMEM((ns, 8, rows), jnp.int32),
        pltpu.VMEM((rows, ns * iface), BF16),
        pltpu.VMEM((ns * iface, rows), BF16),
        pltpu.VMEM((nl, nm, own, rows), F32),
        pltpu.VMEM((nl, nm, own, rows), BF16),
        pltpu.VMEM((nl, own, rows), BF16),
        pltpu.VMEM((nl, own, rows), BF16),
        pltpu.VMEM((nl, own, rows), BF16),
        pltpu.VMEM((nl, nm, own, rows), BF16),
        pltpu.VMEM((nl, nm, own, cols), BF16),
        pltpu.VMEM((nl, nm, own, cols), BF16),
        dma((6,)),
        dma((2, leaves)),
        dma((ns,)), dma((ns,)),
        dma((nl,)), dma((nl,)),
        dma((ns,)), dma((ns,)),
        dma((ns,)), dma((ns,)),
        dma((nl,)), dma((nl,)),
        dma((nl,)), dma((nl,)),
        dma((nl,)), dma((nl,)),
        dma((nl + 1,)), dma((nl + 1,)),
        dma, dma,
    ]
    return pl.pallas_call(
        functools.partial(kernel, nl, ns),
        out_shape=(
            jax.ShapeDtypeStruct((1, own, cols), BF16),
            jax.ShapeDtypeStruct((1, steps, cols), F32),
        ),
        in_specs=[hbm] * 8,
        out_specs=(vmem, vmem),
        scratch_shapes=scratch,
        compiler_params=pltpu.CompilerParams(
            collective_id=0, has_side_effects=True, vmem_limit_bytes=60 * 1024 * 1024
        ),
    )(
        separator_of.reshape(leaves), row_offset, modes, coupling, eigenvalues,
        jnp.swapaxes(stiffness, 1, 2), start_block, rotations,
    )


def solution(mesh):
    in_specs = (
        P(("leaf", "sep"), "mode", None),
        P(("leaf", "sep"), "mode", None),
        P(("leaf", "sep"), "mode"),
        P(("leaf", "sep"), None),
        P(("leaf", "sep")),
        P("sep", None, ("leaf", "mode")),
        P("sep", ("leaf", "mode"), None),
        P("sep", None, None, None),
    )
    out_specs = (P("sep", ("leaf", "mode"), None), P("sep", None, None))
    shape = mesh.shape
    return jax.shard_map(
        functools.partial(per_device, shape["leaf"], shape["sep"], shape["mode"]),
        mesh=mesh, in_specs=in_specs, out_specs=out_specs, check_vma=False,
    )
```

```python
import functools

import jax
import jax.numpy as jnp
from jax import lax
from jax.experimental import pallas as pl
from jax.experimental.pallas import tpu as pltpu
from jax.sharding import PartitionSpec as P

CAP = 2
EPSILON = 1e-06
MESH = pl.DeviceIdType.MESH
F32 = jnp.float32
BF16 = jnp.bfloat16


def remote(src, dst, send_sem, recv_sem, **device):
    return pltpu.make_async_remote_copy(
        src_ref=src,
        dst_ref=dst,
        send_sem=send_sem,
        recv_sem=recv_sem,
        device_id=device,
        device_id_type=MESH,
    )


def contract(a, b, dim_a, dim_b):
    return lax.dot_general(a, b, (((dim_a,), (dim_b,)), ((), ())), preferred_element_type=F32)


def partner(me, distance, count):
    if count & (count - 1):
        return lax.rem(me + distance, count)
    total = jnp.int32(0)
    bit = 1
    while bit < count:
        total = total + (me // bit + distance // bit) % 2 * bit
        bit *= 2
    return total


def kernel(
    nl, ns,
    separator_of, row_offset, modes_hbm, coupling_hbm, eigenvalues_hbm, stiffness_hbm, start_hbm, rotations_hbm,
    out, norms,
    targets, starts, eigenvalues, stiffness, start_block, rotations,
    modes, coupling, eigen_both, part_send, part_recv, scales,
    slot_send, slot_recv, offset_send, offset_recv, placed, places,
    gram, gram_send, gram_recv, leaf_send, leaf_recv, operator, block, normed_rows,
    small_sem, hbm_sem, part_ssem, part_rsem, block_ssem, block_rsem, slot_ssem, slot_rsem,
    offset_ssem, offset_rsem, gram_ssem, gram_rsem, leaf_ssem, leaf_rsem, oper_ssem, oper_rsem,
    core_ssem, core_rsem, eigen_ssem, eigen_rsem,
):
    leaf, sep, core = lax.axis_index("leaf"), lax.axis_index("sep"), lax.axis_index("mode")
    other = 1 - core
    leaves = modes.shape[0]
    iface = coupling.shape[2]
    tile = iface // 2
    half = eigenvalues.shape[1]
    rows = placed.shape[0]
    own, cols = start_block.shape[1:]

    smalls = []
    for k, (src, dst) in enumerate((
        (separator_of, targets), (row_offset, starts), (start_hbm, start_block),
        (eigenvalues_hbm, eigenvalues), (stiffness_hbm, stiffness), (rotations_hbm, rotations),
    )):
        copy = pltpu.make_async_copy(src, dst, small_sem.at[k])
        copy.start()
        smalls.append(copy)
    loads = []
    for l in range(leaves):
        for k, (src, dst) in enumerate(((modes_hbm, modes), (coupling_hbm, coupling))):
            copy = pltpu.make_async_copy(src.at[l], dst.at[l], hbm_sem.at[k, l])
            copy.start()
            loads.append(copy)

    barrier = pltpu.get_barrier_semaphore()
    pl.semaphore_signal(barrier, inc=1, device_id={"mode": other}, device_id_type=MESH)
    for d in range(1, ns):
        pl.semaphore_signal(
            barrier, inc=1, device_id={"sep": partner(sep, d, ns)}, device_id_type=MESH
        )
    for d in range(1, nl):
        pl.semaphore_signal(
            barrier, inc=1, device_id={"leaf": lax.rem(leaf + d, nl)}, device_id_type=MESH
        )
    smalls[0].wait()
    smalls[1].wait()

    target = [targets[l] for l in range(leaves)]
    position = []
    for l in range(leaves):
        count = jnp.int32(0)
        for e in range(l):
            count = count + jnp.where(target[e] == target[l], 1, 0)
        position.append(count)
    order = list(range(ns // 2, ns)) + list(range(1, ns // 2)) + [0]
    slots = []
    for d in order:
        owner = partner(sep, d, ns)
        found = []
        for p in (other, core):
            index = jnp.int32(0)
            offset = jnp.int32(-4 * rows)
            for l in range(leaves):
                mine = (target[l] == owner) & (position[l] == p)
                index = jnp.where(mine, l, index)
                offset = jnp.where(mine, starts[l], offset)
            found.append(index)
        offset_send[d] = jnp.full(offset_send.shape[1:], offset, jnp.int32)
        slots.append((d, owner, found[0], found[1]))
    pl.semaphore_wait(barrier, 1 + (ns - 1) + (nl - 1))
    offset_copies = {}
    for d in order[:-1]:
        copy = remote(
            offset_send.at[d], offset_recv.at[d], offset_ssem.at[d], offset_rsem.at[d],
            sep=partner(sep, d, ns),
        )
        copy.start()
        offset_copies[d] = copy

    smalls[2].wait()
    block[leaf, core] = start_block[0]
    block_copies = []
    for d in range(1, nl):
        copy = remote(
            start_block.at[0], block.at[leaf, core], block_ssem.at[d], block_rsem.at[d],
            leaf=lax.rem(leaf + d, nl),
        )
        copy.start()
        block_copies.append(copy)

    smalls[3].wait()
    eigen_both[core] = eigenvalues[...]
    eigen_copy = remote(eigenvalues, eigen_both.at[core], eigen_ssem, eigen_rsem, mode=other)
    eigen_copy.start()

    for copy in loads:
        copy.wait()
    eigen_copy.wait()
    for k in range(2):
        scales[:, k * half:(k + 1) * half] = 1.0 / jnp.sqrt(eigen_both[k])
    slot_copies = {}
    part_copies = {}

    def give(d, owner, given, kept):
        part_send[d] = contract(coupling[given], modes[given], 0, 0).astype(BF16)
        copy = remote(part_send.at[d], part_recv.at[d], part_ssem.at[d], part_rsem.at[d], mode=other)
        copy.start()
        part_copies[d] = copy

    give(*slots[0])
    for step, (d, owner, given, kept) in enumerate(slots):
        product = contract(coupling[kept], modes[kept], 0, 0)
        if step + 1 < len(slots):
            give(*slots[step + 1])
        part_copies[d].wait()
        scaled = ((product + part_recv[d].astype(F32)) * scales[pl.ds(kept, 1), :]).astype(BF16)
        square = contract(scaled, scaled, 1, 1).astype(BF16)
        slot_send[d, 0] = square[:tile, :tile]
        slot_send[d, 1] = square[tile:, :tile]
        slot_send[d, 2] = square[tile:, tile:]
        if d > 0:
            copy = remote(slot_send.at[d], slot_recv.at[d], slot_ssem.at[d], slot_rsem.at[d], sep=owner)
            copy.start()
            slot_copies[d] = copy

    for copy in block_copies:
        copy.wait()
    block_core = remote(
        block.at[:, core], block.at[:, core], core_ssem.at[nl], core_rsem.at[nl], mode=other
    )
    block_core.start()

    shift = lax.broadcasted_iota(jnp.int32, (rows, iface), 0) - lax.broadcasted_iota(
        jnp.int32, (rows, iface), 1
    )
    turned_shift = lax.broadcasted_iota(jnp.int32, (iface, rows), 1) - lax.broadcasted_iota(
        jnp.int32, (iface, rows), 0
    )
    for d in [0] + order[:-1]:
        blocks, offsets = (slot_send, offset_send) if d == 0 else (slot_recv, offset_recv)
        if d > 0:
            offset_copies[d].wait()
        place = jnp.where(shift == offsets[d, 0:1, :iface], 1.0, 0.0).astype(BF16)
        places[d * iface:(d + 1) * iface, :] = jnp.where(
            turned_shift == offsets[d, 0:1, :], 1.0, 0.0
        ).astype(BF16)
        if d > 0:
            slot_copies[d].wait()
        corner = blocks[d, 1]
        top = jnp.concatenate([blocks[d, 0], corner.T], axis=1)
        low = jnp.concatenate([corner, blocks[d, 2]], axis=1)
        placed[:, d * iface:(d + 1) * iface] = (
            jnp.dot(place[:, :tile], top, preferred_element_type=F32)
            + jnp.dot(place[:, tile:], low, preferred_element_type=F32)
        ).astype(BF16)

    gram_copies = []
    peers = [lax.rem(leaf + d, nl) for d in list(range(1, nl)) + [0]]
    pair_rows = 2 * own
    for d, peer in enumerate(peers):
        chunk = placed[pl.ds(pl.multiple_of(peer * pair_rows, pair_rows), pair_rows), :]
        product = jnp.dot(chunk, places[...], preferred_element_type=F32).reshape(2, own, rows)
        gram[d] = product
        gram_send[d] = product.astype(BF16)
        copy = remote(
            gram_send.at[d, other], gram_recv.at[d], gram_ssem.at[d], gram_rsem.at[d], mode=other
        )
        copy.start()
        gram_copies.append(copy)
    leaf_copies = []
    for d, peer in enumerate(peers[:-1]):
        gram_copies[d].wait()
        leaf_send[d] = (gram[d, core] + gram_recv[d].astype(F32)).astype(BF16)
        copy = remote(leaf_send.at[d], leaf_recv.at[d], leaf_ssem.at[d], leaf_rsem.at[d], leaf=peer)
        copy.start()
        leaf_copies.append(copy)
    smalls[4].wait()
    gram_copies[nl - 1].wait()
    total = stiffness[0].astype(F32) - (gram[nl - 1, core] + gram_recv[nl - 1].astype(F32))
    for d in range(nl - 1):
        leaf_copies[d].wait()
        total = total - leaf_recv[d].astype(F32)
    operator[leaf, core] = total.astype(BF16)

    oper_copies = []
    for d in range(1, nl):
        copy = remote(
            operator.at[leaf, core], operator.at[leaf, core], oper_ssem.at[d], oper_rsem.at[d],
            leaf=lax.rem(leaf + d, nl),
        )
        copy.start()
        oper_copies.append(copy)
    core_copies = []
    for d in range(nl):
        if d > 0:
            oper_copies[d - 1].wait()
        source = lax.rem(leaf - d + nl, nl)
        copy = remote(
            operator.at[source, core], operator.at[source, core], core_ssem.at[d], core_rsem.at[d], mode=other
        )
        copy.start()
        core_copies.append(copy)
    block_core.wait()
    smalls[5].wait()
    for copy in core_copies:
        copy.wait()

    turned = operator[...].reshape(rows, rows).T
    current = block[...].reshape(rows, cols)
    steps = rotations.shape[1]
    for k in range(steps):
        result = jnp.dot(turned, current, preferred_element_type=F32)
        square_sums = jnp.sum(result * result, 0, keepdims=True)
        norms[0, k:k + 1, :] = square_sums
        column_scale = jnp.sqrt(square_sums / rows + EPSILON)
        normed = (result * (1.0 / column_scale)).astype(BF16)
        if k < steps - 1:
            current = jnp.dot(normed, rotations[0, k], preferred_element_type=F32).astype(BF16)
        else:
            normed_rows[...] = normed.reshape(normed_rows.shape)
            out[0] = normed_rows[leaf, core]


def per_device(nl, ns, nm, modes, coupling, eigenvalues, separator_of, row_offset, stiffness, start_block, rotations):
    leaves, depth, width = modes.shape
    iface = coupling.shape[2]
    half = eigenvalues.shape[1]
    rows = stiffness.shape[1]
    own, cols = start_block.shape[1:]
    steps = rotations.shape[1]
    vmem = pl.BlockSpec(memory_space=pltpu.VMEM)
    hbm = pl.BlockSpec(memory_space=pl.ANY)
    dma = pltpu.SemaphoreType.DMA
    assert nm == CAP
    scratch = [
        pltpu.SMEM((leaves,), jnp.int32),
        pltpu.SMEM((leaves,), jnp.int32),
        pltpu.VMEM((leaves, half), F32),
        pltpu.VMEM((1, own, rows), BF16),
        pltpu.VMEM((1, own, cols), BF16),
        pltpu.VMEM((1, steps, cols, cols), BF16),
        pltpu.VMEM((leaves, depth, width), BF16),
        pltpu.VMEM((leaves, depth, iface), BF16),
        pltpu.VMEM((nm, leaves, half), F32),
        pltpu.VMEM((ns, iface, width), BF16),
        pltpu.VMEM((ns, iface, width), BF16),
        pltpu.VMEM((leaves, width), F32),
        pltpu.VMEM((ns, 3, iface // 2, iface // 2), BF16),
        pltpu.VMEM((ns, 3, iface // 2, iface // 2), BF16),
        pltpu.VMEM((ns, 8, rows), jnp.int32),
        pltpu.VMEM((ns, 8, rows), jnp.int32),
        pltpu.VMEM((rows, ns * iface), BF16),
        pltpu.VMEM((ns * iface, rows), BF16),
        pltpu.VMEM((nl, nm, own, rows), F32),
        pltpu.VMEM((nl, nm, own, rows), BF16),
        pltpu.VMEM((nl, own, rows), BF16),
        pltpu.VMEM((nl, own, rows), BF16),
        pltpu.VMEM((nl, own, rows), BF16),
        pltpu.VMEM((nl, nm, own, rows), BF16),
        pltpu.VMEM((nl, nm, own, cols), BF16),
        pltpu.VMEM((nl, nm, own, cols), BF16),
        dma((6,)),
        dma((2, leaves)),
        dma((ns,)), dma((ns,)),
        dma((nl,)), dma((nl,)),
        dma((ns,)), dma((ns,)),
        dma((ns,)), dma((ns,)),
        dma((nl,)), dma((nl,)),
        dma((nl,)), dma((nl,)),
        dma((nl,)), dma((nl,)),
        dma((nl + 1,)), dma((nl + 1,)),
        dma, dma,
    ]
    normed, square_sums = pl.pallas_call(
        functools.partial(kernel, nl, ns),
        out_shape=(
            jax.ShapeDtypeStruct((1, own, cols), BF16),
            jax.ShapeDtypeStruct((1, steps, cols), F32),
        ),
        in_specs=[hbm] * 8,
        out_specs=(vmem, vmem),
        scratch_shapes=scratch,
        compiler_params=pltpu.CompilerParams(
            collective_id=0, has_side_effects=True, vmem_limit_bytes=60 * 1024 * 1024
        ),
    )(
        separator_of.reshape(leaves), row_offset, modes, coupling, eigenvalues,
        jnp.swapaxes(stiffness, 1, 2), start_block, rotations,
    )
    subspace = jnp.dot(normed[0], rotations[0, steps - 1], preferred_element_type=F32)
    return subspace.astype(BF16)[None], jnp.sqrt(square_sums / rows + EPSILON)


def solution(mesh):
    in_specs = (
        P(("leaf", "sep"), "mode", None),
        P(("leaf", "sep"), "mode", None),
        P(("leaf", "sep"), "mode"),
        P(("leaf", "sep"), None),
        P(("leaf", "sep")),
        P("sep", None, ("leaf", "mode")),
        P("sep", ("leaf", "mode"), None),
        P("sep", None, None, None),
    )
    out_specs = (P("sep", ("leaf", "mode"), None), P("sep", None, None))
    shape = mesh.shape
    return jax.shard_map(
        functools.partial(per_device, shape["leaf"], shape["sep"], shape["mode"]),
        mesh=mesh, in_specs=in_specs, out_specs=out_specs, check_vma=False,
    )
```

```python
import functools

import jax
import jax.numpy as jnp
from jax import lax
from jax.experimental import pallas as pl
from jax.experimental.pallas import tpu as pltpu
from jax.sharding import PartitionSpec as P

CAP = 2
EPSILON = 1e-06
MESH = pl.DeviceIdType.MESH
F32 = jnp.float32
BF16 = jnp.bfloat16


def remote(src, dst, send_sem, recv_sem, **device):
    return pltpu.make_async_remote_copy(
        src_ref=src,
        dst_ref=dst,
        send_sem=send_sem,
        recv_sem=recv_sem,
        device_id=device,
        device_id_type=MESH,
    )


def contract(a, b, dim_a, dim_b):
    return lax.dot_general(a, b, (((dim_a,), (dim_b,)), ((), ())), preferred_element_type=F32)


def partner(me, distance, count):
    if count & (count - 1):
        return lax.rem(me + distance, count)
    total = jnp.int32(0)
    bit = 1
    while bit < count:
        total = total + (me // bit + distance // bit) % 2 * bit
        bit *= 2
    return total


def kernel(
    nl, ns,
    separator_of, row_offset, modes_hbm, coupling_hbm, eigenvalues_hbm, stiffness_hbm, start_hbm, rotations_hbm,
    out, norms,
    targets, starts, eigenvalues, stiffness, start_block, rotations,
    modes, coupling, eigen_both, part_send, part_recv, scales,
    slot_send, slot_recv, offset_send, offset_recv, placed, places,
    gram, gram_send, gram_recv, leaf_send, leaf_recv, operator, block, normed_rows,
    small_sem, hbm_sem, part_ssem, part_rsem, block_ssem, block_rsem, slot_ssem, slot_rsem,
    offset_ssem, offset_rsem, gram_ssem, gram_rsem, leaf_ssem, leaf_rsem, oper_ssem, oper_rsem,
    core_ssem, core_rsem, eigen_ssem, eigen_rsem,
):
    leaf, sep, core = lax.axis_index("leaf"), lax.axis_index("sep"), lax.axis_index("mode")
    other = 1 - core
    leaves = modes.shape[0]
    iface = coupling.shape[2]
    tile = iface // 2
    half = eigenvalues.shape[1]
    rows = placed.shape[0]
    own, cols = start_block.shape[1:]

    barrier = pltpu.get_barrier_semaphore()
    pl.semaphore_signal(barrier, inc=1, device_id={"mode": other}, device_id_type=MESH)
    for d in range(1, ns):
        pl.semaphore_signal(
            barrier, inc=1, device_id={"sep": partner(sep, d, ns)}, device_id_type=MESH
        )
    for d in range(1, nl):
        pl.semaphore_signal(
            barrier, inc=1, device_id={"leaf": lax.rem(leaf + d, nl)}, device_id_type=MESH
        )

    smalls = []
    for k, (src, dst) in enumerate((
        (separator_of, targets), (row_offset, starts), (start_hbm, start_block),
        (eigenvalues_hbm, eigenvalues), (stiffness_hbm, stiffness), (rotations_hbm, rotations),
    )):
        copy = pltpu.make_async_copy(src, dst, small_sem.at[k])
        copy.start()
        smalls.append(copy)
    loads = []
    step = leaves // 2
    for l in range(2):
        for k, (src, dst) in enumerate(((modes_hbm, modes), (coupling_hbm, coupling))):
            part = pl.ds(l * step, step)
            copy = pltpu.make_async_copy(src.at[part], dst.at[part], hbm_sem.at[k, l])
            copy.start()
            loads.append(copy)

    smalls[0].wait()
    smalls[1].wait()

    target = [targets[l] for l in range(leaves)]
    position = []
    for l in range(leaves):
        count = jnp.int32(0)
        for e in range(l):
            count = count + jnp.where(target[e] == target[l], 1, 0)
        position.append(count)
    order = list(range(ns // 2, ns)) + list(range(1, ns // 2)) + [0]
    slots = []
    for d in order:
        owner = partner(sep, d, ns)
        found = []
        for p in (other, core):
            index = jnp.int32(0)
            offset = jnp.int32(-4 * rows)
            for l in range(leaves):
                mine = (target[l] == owner) & (position[l] == p)
                index = jnp.where(mine, l, index)
                offset = jnp.where(mine, starts[l], offset)
            found.append(index)
        offset_send[d] = jnp.full(offset_send.shape[1:], offset, jnp.int32)
        slots.append((d, owner, found[0], found[1]))
    pl.semaphore_wait(barrier, 1 + (ns - 1) + (nl - 1))
    offset_copies = {}
    for d in order[:-1]:
        copy = remote(
            offset_send.at[d], offset_recv.at[d], offset_ssem.at[d], offset_rsem.at[d],
            sep=partner(sep, d, ns),
        )
        copy.start()
        offset_copies[d] = copy

    smalls[2].wait()
    block[leaf, core] = start_block[0]
    block_copies = []
    for d in range(1, nl):
        copy = remote(
            start_block.at[0], block.at[leaf, core], block_ssem.at[d], block_rsem.at[d],
            leaf=lax.rem(leaf + d, nl),
        )
        copy.start()
        block_copies.append(copy)

    smalls[3].wait()
    eigen_both[core] = eigenvalues[...]
    eigen_copy = remote(eigenvalues, eigen_both.at[core], eigen_ssem, eigen_rsem, mode=other)
    eigen_copy.start()

    for copy in loads:
        copy.wait()
    eigen_copy.wait()
    for k in range(2):
        scales[:, k * half:(k + 1) * half] = 1.0 / jnp.sqrt(eigen_both[k])
    slot_copies = {}
    part_copies = {}

    def give(d, owner, given, kept):
        part_send[d] = contract(coupling[given], modes[given], 0, 0).astype(BF16)
        copy = remote(part_send.at[d], part_recv.at[d], part_ssem.at[d], part_rsem.at[d], mode=other)
        copy.start()
        part_copies[d] = copy

    give(*slots[0])
    for step, (d, owner, given, kept) in enumerate(slots):
        product = contract(coupling[kept], modes[kept], 0, 0)
        if step + 1 < len(slots):
            give(*slots[step + 1])
        part_copies[d].wait()
        scaled = ((product + part_recv[d].astype(F32)) * scales[pl.ds(kept, 1), :]).astype(BF16)
        square = contract(scaled, scaled, 1, 1).astype(BF16)
        slot_send[d, 0] = square[:tile, :tile]
        slot_send[d, 1] = square[tile:, :tile]
        slot_send[d, 2] = square[tile:, tile:]
        if d > 0:
            copy = remote(slot_send.at[d], slot_recv.at[d], slot_ssem.at[d], slot_rsem.at[d], sep=owner)
            copy.start()
            slot_copies[d] = copy

    for copy in block_copies:
        copy.wait()
    block_core = remote(
        block.at[:, core], block.at[:, core], core_ssem.at[nl], core_rsem.at[nl], mode=other
    )
    block_core.start()

    shift = lax.broadcasted_iota(jnp.int32, (rows, iface), 0) - lax.broadcasted_iota(
        jnp.int32, (rows, iface), 1
    )
    turned_shift = lax.broadcasted_iota(jnp.int32, (iface, rows), 1) - lax.broadcasted_iota(
        jnp.int32, (iface, rows), 0
    )
    for d in [0] + order[:-1]:
        blocks, offsets = (slot_send, offset_send) if d == 0 else (slot_recv, offset_recv)
        if d > 0:
            offset_copies[d].wait()
        place = jnp.where(shift == offsets[d, 0:1, :iface], 1.0, 0.0).astype(BF16)
        places[d * iface:(d + 1) * iface, :] = jnp.where(
            turned_shift == offsets[d, 0:1, :], 1.0, 0.0
        ).astype(BF16)
        if d > 0:
            slot_copies[d].wait()
        corner = blocks[d, 1]
        top = jnp.concatenate([blocks[d, 0], corner.T], axis=1)
        low = jnp.concatenate([corner, blocks[d, 2]], axis=1)
        placed[:, d * iface:(d + 1) * iface] = (
            jnp.dot(place[:, :tile], top, preferred_element_type=F32)
            + jnp.dot(place[:, tile:], low, preferred_element_type=F32)
        ).astype(BF16)

    gram_copies = []
    peers = [lax.rem(leaf + d, nl) for d in list(range(1, nl)) + [0]]
    pair_rows = 2 * own
    for d, peer in enumerate(peers):
        chunk = placed[pl.ds(pl.multiple_of(peer * pair_rows, pair_rows), pair_rows), :]
        product = jnp.dot(chunk, places[...], preferred_element_type=F32).reshape(2, own, rows)
        gram[d] = product
        gram_send[d] = product.astype(BF16)
        copy = remote(
            gram_send.at[d, other], gram_recv.at[d], gram_ssem.at[d], gram_rsem.at[d], mode=other
        )
        copy.start()
        gram_copies.append(copy)
    leaf_copies = []
    for d, peer in enumerate(peers[:-1]):
        gram_copies[d].wait()
        leaf_send[d] = (gram[d, core] + gram_recv[d].astype(F32)).astype(BF16)
        copy = remote(leaf_send.at[d], leaf_recv.at[d], leaf_ssem.at[d], leaf_rsem.at[d], leaf=peer)
        copy.start()
        leaf_copies.append(copy)
    smalls[4].wait()
    gram_copies[nl - 1].wait()
    total = stiffness[0].astype(F32) - (gram[nl - 1, core] + gram_recv[nl - 1].astype(F32))
    for d in range(nl - 1):
        leaf_copies[d].wait()
        total = total - leaf_recv[d].astype(F32)
    operator[leaf, core] = total.astype(BF16)

    oper_copies = []
    for d in range(1, nl):
        copy = remote(
            operator.at[leaf, core], operator.at[leaf, core], oper_ssem.at[d], oper_rsem.at[d],
            leaf=lax.rem(leaf + d, nl),
        )
        copy.start()
        oper_copies.append(copy)
    core_copies = []
    for d in range(nl):
        if d > 0:
            oper_copies[d - 1].wait()
        source = lax.rem(leaf - d + nl, nl)
        copy = remote(
            operator.at[source, core], operator.at[source, core], core_ssem.at[d], core_rsem.at[d], mode=other
        )
        copy.start()
        core_copies.append(copy)
    block_core.wait()
    smalls[5].wait()
    for copy in core_copies:
        copy.wait()

    turned = operator[...].reshape(rows, rows).T
    current = block[...].reshape(rows, cols)
    steps = rotations.shape[1]
    for k in range(steps):
        result = jnp.dot(turned, current, preferred_element_type=F32)
        column_scale = jnp.sqrt(jnp.sum(result * result, 0, keepdims=True) / rows + EPSILON)
        norms[0, k:k + 1, :] = column_scale
        normed = (result * (1.0 / column_scale)).astype(BF16)
        if k < steps - 1:
            current = jnp.dot(normed, rotations[0, k], preferred_element_type=F32).astype(BF16)
        else:
            normed_rows[...] = normed.reshape(normed_rows.shape)
            out[0] = jnp.dot(
                normed_rows[leaf, core], rotations[0, k], preferred_element_type=F32
            ).astype(BF16)


def per_device(nl, ns, nm, modes, coupling, eigenvalues, separator_of, row_offset, stiffness, start_block, rotations):
    leaves, depth, width = modes.shape
    iface = coupling.shape[2]
    half = eigenvalues.shape[1]
    rows = stiffness.shape[1]
    own, cols = start_block.shape[1:]
    steps = rotations.shape[1]
    vmem = pl.BlockSpec(memory_space=pltpu.VMEM)
    hbm = pl.BlockSpec(memory_space=pl.ANY)
    dma = pltpu.SemaphoreType.DMA
    assert nm == CAP
    scratch = [
        pltpu.SMEM((leaves,), jnp.int32),
        pltpu.SMEM((leaves,), jnp.int32),
        pltpu.VMEM((leaves, half), F32),
        pltpu.VMEM((1, own, rows), BF16),
        pltpu.VMEM((1, own, cols), BF16),
        pltpu.VMEM((1, steps, cols, cols), BF16),
        pltpu.VMEM((leaves, depth, width), BF16),
        pltpu.VMEM((leaves, depth, iface), BF16),
        pltpu.VMEM((nm, leaves, half), F32),
        pltpu.VMEM((ns, iface, width), BF16),
        pltpu.VMEM((ns, iface, width), BF16),
        pltpu.VMEM((leaves, width), F32),
        pltpu.VMEM((ns, 3, iface // 2, iface // 2), BF16),
        pltpu.VMEM((ns, 3, iface // 2, iface // 2), BF16),
        pltpu.VMEM((ns, 8, rows), jnp.int32),
        pltpu.VMEM((ns, 8, rows), jnp.int32),
        pltpu.VMEM((rows, ns * iface), BF16),
        pltpu.VMEM((ns * iface, rows), BF16),
        pltpu.VMEM((nl, nm, own, rows), F32),
        pltpu.VMEM((nl, nm, own, rows), BF16),
        pltpu.VMEM((nl, own, rows), BF16),
        pltpu.VMEM((nl, own, rows), BF16),
        pltpu.VMEM((nl, own, rows), BF16),
        pltpu.VMEM((nl, nm, own, rows), BF16),
        pltpu.VMEM((nl, nm, own, cols), BF16),
        pltpu.VMEM((nl, nm, own, cols), BF16),
        dma((6,)),
        dma((2, 2)),
        dma((ns,)), dma((ns,)),
        dma((nl,)), dma((nl,)),
        dma((ns,)), dma((ns,)),
        dma((ns,)), dma((ns,)),
        dma((nl,)), dma((nl,)),
        dma((nl,)), dma((nl,)),
        dma((nl,)), dma((nl,)),
        dma((nl + 1,)), dma((nl + 1,)),
        dma, dma,
    ]
    return pl.pallas_call(
        functools.partial(kernel, nl, ns),
        out_shape=(
            jax.ShapeDtypeStruct((1, own, cols), BF16),
            jax.ShapeDtypeStruct((1, steps, cols), F32),
        ),
        in_specs=[hbm] * 8,
        out_specs=(vmem, vmem),
        scratch_shapes=scratch,
        compiler_params=pltpu.CompilerParams(
            collective_id=0, has_side_effects=True, vmem_limit_bytes=60 * 1024 * 1024
        ),
    )(
        separator_of.reshape(leaves), row_offset, modes, coupling, eigenvalues,
        jnp.swapaxes(stiffness, 1, 2), start_block, rotations,
    )


def solution(mesh):
    in_specs = (
        P(("leaf", "sep"), "mode", None),
        P(("leaf", "sep"), "mode", None),
        P(("leaf", "sep"), "mode"),
        P(("leaf", "sep"), None),
        P(("leaf", "sep")),
        P("sep", None, ("leaf", "mode")),
        P("sep", ("leaf", "mode"), None),
        P("sep", None, None, None),
    )
    out_specs = (P("sep", ("leaf", "mode"), None), P("sep", None, None))
    shape = mesh.shape
    return jax.shard_map(
        functools.partial(per_device, shape["leaf"], shape["sep"], shape["mode"]),
        mesh=mesh, in_specs=in_specs, out_specs=out_specs, check_vma=False,
    )
```
